32 devices in a mesh: seq: 16 (over z, y, core), exp: 2 (over x).
Axes of the slice: x: 2, y: 2, z: 4, core: 2. Of those that a mesh axis runs over, the one named last changes fastest.
Arguments:
- tokens: bfloat16 [2048, 2880], P('seq'), may hold values from -6 to 6
- expert_ids: int32 [2048, 4], P('seq'), may hold values from 0 to 15, all different within a row; in each aligned block of 128 rows (0 to 127, 128 to 255, ...) at most 48 rows name the same one
- route_weights: float32 [2048, 4], P('seq'), may hold values from 0.05 to 1
- cotangent: bfloat16 [2048, 2880], P('seq'), may hold values from -3 to 3
- w_gate: bfloat16 [16, 2880, 2048], P('seq', None, 'exp'), may hold values from -0.109375 to 0.109375
- w_up: bfloat16 [16, 2880, 2048], P('seq', None, 'exp'), may hold values from -0.109375 to 0.109375
- w_down: bfloat16 [16, 2048, 2880], P('seq', 'exp'), may hold values from -0.125 to 0.125
Outputs:
- moe_out: bfloat16 [2048, 2880], P('seq')
- token_grad: bfloat16 [2048, 2880], P('seq')
- weight_grad: float32 [2048, 4], P('seq')
- gate_proj_grad: bfloat16 [16, 2880, 2048], P('seq', None, 'exp')
- up_proj_grad: bfloat16 [16, 2880, 2048], P('seq', None, 'exp')
- down_proj_grad: bfloat16 [16, 2048, 2880], P('seq', 'exp')
The draws below stay inside these ranges and needn't reach their ends.
Inputs may be any that keep to these rules, and one draw needn't show every extreme that they name: `expert_ids`: within the tokens of one slab (128 rows) no expert is named by more than 48 routes, a bound that some block reaches; the 4 ids of a row differ.
All inputs are finite; a program needn't handle non-finite values.
Results may differ from the reference program's by a relative error of at most 0.0058.
Values may be sent and summed in bfloat16 or wider, within the bound.
A program may use at most 256 MiB of HBM per device.

```python
import math
import jax
import jax.numpy as jnp
import numpy as np
from jax import lax

D = 2880
FF = 2048
TOP = 4
TOK_SEQ = 128
TOKENS = 2048
EXPERTS = 16
CAP = 48
N_SEQ = 16


def steps_of(stream_key, extent, pieces, smallest, largest):
    level, own = 1.0, jax.random.fold_in(stream_key, 6)
    for position, blocks in pieces:
        draws = jnp.exp(jax.random.uniform(jax.random.fold_in(own, position), (blocks,), jnp.float32, smallest / len(pieces), largest / len(pieces)))
        level = level * jnp.repeat(draws, extent[position] // blocks).reshape([-1 if axis == position else 1 for axis in range(len(extent))])
    return level


def shared_out(rng, own, number, rows, count, top, bound, skew):
    order = jax.random.permutation(rng, count)
    packed, usual = load_shares(count, rows * top, bound, skew, True), load_shares(count, rows * top, bound, skew, False)
    places = jnp.arange(count)

    def named(tallies, offset_by):
        used = int((tallies > 0).sum())
        fixed = max(1, used // 4)
        moved = fixed + (places - fixed + offset_by * (used - fixed)) % max(1, count - fixed)
        return jnp.zeros((count,), jnp.int32).at[order[jnp.where(places < fixed, places, moved)]].set(jnp.asarray(tallies, jnp.int32))

    tallies = jnp.where(number % 4 == 0, named(packed, number // 4), named(usual, number - number // 4 - 1))
    mixed = jax.random.permutation(jax.random.fold_in(own, 3), count)
    donor, sink = mixed[0:count // 2 * 2:2], mixed[1:count // 2 * 2:2]
    room = jnp.minimum(tallies[donor] - 1, bound - tallies[sink]) // 2
    room = jnp.where((donor == order[0]) | (sink == order[0]) | (tallies[sink] == 0), 0, jnp.maximum(room, 0))
    moved = jax.random.randint(jax.random.fold_in(own, 4), (count // 2,), 0, 1 << 20) % (room + 1)
    tallies = tallies.at[donor].add(-moved).at[sink].add(moved)
    labels = jnp.searchsorted(jnp.cumsum(tallies), jnp.arange(rows * top), side="right").astype(jnp.int32)
    listing = labels.reshape(top, rows).T
    listing = listing[jax.random.permutation(jax.random.fold_in(own, 1), rows)]
    offset_by = jax.random.randint(jax.random.fold_in(own, 2), (rows, 1), 0, top)
    return jnp.take_along_axis(listing, (jnp.arange(top)[None, :] + offset_by) % top, axis=1)


def load_shares(count, total, bound, slope, full):
    loads = [(1 << 20) // math.isqrt(grade ** slope) + 1 for grade in range(1, count + 1)]
    largest = bound if full else min(bound, max(-(-total // count), total * loads[0] // sum(loads)))
    least = 1 if total - largest >= count - 1 else 0
    counts, rest = [largest] + [least] * (count - 1), total - largest - least * (count - 1)
    while rest > 0:
        free = [i for i in range(1, count) if counts[i] < largest] or [i for i in range(1, count) if counts[i] < bound]
        whole, budget = sum([loads[i] for i in free]), rest
        for i in free:
            addition = min(bound - counts[i], max(1, budget * loads[i] // whole), rest)
            counts[i] = counts[i] + addition
            rest = rest - addition
    return np.array(counts)


def gaussian(rng, shape, deviation, most, split=(), kind=jnp.bfloat16):
    gain = steps_of(rng, shape, split, -0.22, 0.18) if split else 1.0
    array = jax.random.normal(rng, shape, jnp.float32) * deviation * gain
    return jnp.minimum(jnp.maximum(array, -most), most).astype(kind)


def setup_inputs(seed: int = 0) -> dict:
    seeds = jax.random.split(jax.random.key(seed), 8)
    tokens = gaussian(seeds[0], (TOKENS, D), 1.0, 6.0, ((0, 16),))
    expert_ids_keys = jax.random.split(jax.random.fold_in(seeds[1], 1), TOKENS // TOK_SEQ)
    expert_ids_turns = jax.random.permutation(jax.random.fold_in(seeds[1], 3), TOKENS // TOK_SEQ)
    expert_ids = jax.vmap(lambda own, number: shared_out(jax.random.fold_in(seeds[1], 2), own, number, TOK_SEQ, EXPERTS, TOP, CAP, 2))(expert_ids_keys, expert_ids_turns).reshape((TOKENS, TOP))
    route_weights = jnp.clip(jnp.exp(math.log(1.0) - 2.9957323 * jax.random.uniform(seeds[2], (TOKENS, TOP), jnp.float32) ** steps_of(seeds[2], (TOKENS, TOP), ((0, 16),), -0.2, 0.2)), 0.05, 1.0)
    cotangent = gaussian(seeds[3], (TOKENS, D), 0.5, 3.0, ((0, 16),))
    w_gate = gaussian(seeds[4], (EXPERTS, D, FF), D ** -0.5, 0.109375, ((0, 16), (2, 2)))
    w_up = gaussian(seeds[5], (EXPERTS, D, FF), D ** -0.5, 0.109375, ((0, 16), (2, 2)))
    w_down = gaussian(seeds[6], (EXPERTS, FF, D), FF ** -0.5, 0.125, ((0, 16), (1, 2)))
    return dict(tokens=tokens, expert_ids=expert_ids, route_weights=route_weights, cotangent=cotangent, w_gate=w_gate, w_up=w_up, w_down=w_down)


def expert_pass(operands):
    x_rows, r_rows, w_gate, w_up, w_down = operands
    gate = jnp.dot(x_rows, w_gate, preferred_element_type=jnp.float32)
    up = jnp.dot(x_rows, w_up, preferred_element_type=jnp.float32)
    sigma = jax.nn.sigmoid(gate)
    silu = gate * sigma
    hidden = (silu * up).astype(jnp.bfloat16)
    y_part = jnp.dot(hidden, w_down, preferred_element_type=jnp.float32)
    d_hidden = jnp.dot(r_rows, w_down.T, preferred_element_type=jnp.float32)
    d_gate = (d_hidden * up * sigma * (1.0 + gate * (1.0 - sigma))).astype(jnp.bfloat16)
    d_up = (d_hidden * silu).astype(jnp.bfloat16)
    dx_part = jnp.dot(d_gate, w_gate.T, preferred_element_type=jnp.float32) + jnp.dot(d_up, w_up.T, preferred_element_type=jnp.float32)
    g_gate = jnp.dot(x_rows.T, d_gate, preferred_element_type=jnp.float32).astype(jnp.bfloat16)
    g_up = jnp.dot(x_rows.T, d_up, preferred_element_type=jnp.float32).astype(jnp.bfloat16)
    g_down = jnp.dot(hidden.T, r_rows, preferred_element_type=jnp.float32).astype(jnp.bfloat16)
    return y_part, dx_part, g_gate, g_up, g_down


def reference(tokens, expert_ids, route_weights, cotangent, w_gate, w_up, w_down):
    rows_all = N_SEQ * CAP
    blocks = expert_ids.reshape(N_SEQ, TOK_SEQ * TOP)
    onehot = (blocks[:, :, None] == jnp.arange(EXPERTS, dtype=jnp.int32)[None, None, :]).astype(jnp.int32)
    slot = jnp.sum((jnp.cumsum(onehot, axis=1) - 1) * onehot, axis=2)
    source = jnp.arange(N_SEQ, dtype=jnp.int32)[:, None]
    target = (blocks * rows_all + source * CAP + slot).reshape(-1).astype(jnp.int32)
    x_routes = jnp.repeat(tokens, TOP, axis=0)
    scaled = (route_weights[:, :, None] * cotangent[:, None, :].astype(jnp.float32)).astype(jnp.bfloat16).reshape(TOKENS * TOP, D)
    x_buf = jnp.zeros((EXPERTS * rows_all, D), jnp.bfloat16).at[target].set(x_routes).reshape(EXPERTS, rows_all, D)
    r_buf = jnp.zeros((EXPERTS * rows_all, D), jnp.bfloat16).at[target].set(scaled).reshape(EXPERTS, rows_all, D)
    y_all, dx_all, g_gate, g_up, g_down = lax.map(expert_pass, (x_buf, r_buf, w_gate, w_up, w_down))
    y_routes = y_all.reshape(EXPERTS * rows_all, D)[target].reshape(TOKENS, TOP, D)
    dx_routes = dx_all.reshape(EXPERTS * rows_all, D)[target].reshape(TOKENS, TOP, D)
    moe_out = jnp.sum(route_weights[:, :, None] * y_routes, axis=1).astype(jnp.bfloat16)
    token_grad = jnp.sum(dx_routes, axis=1).astype(jnp.bfloat16)
    weight_grad = jnp.sum(y_routes * cotangent[:, None, :].astype(jnp.float32), axis=2)
    return moe_out, token_grad, weight_grad, g_gate, g_up, g_down
```

```python
import jax
import jax.numpy as jnp
from jax import lax
from jax.sharding import PartitionSpec as P


def dot(left, right, dims):
    return lax.dot_general(left, right, (dims, ((), ())), preferred_element_type=jnp.float32)


def body(tokens, expert_ids, route_weights, cotangent, w_gate, w_up, w_down):
    tok, width = tokens.shape
    top = expert_ids.shape[1]
    experts = lax.axis_size("seq")
    shares = lax.axis_size("exp")
    rows = 3 * tok * top // 2
    share = tok // shares
    me = lax.axis_index("seq")
    mine = lax.axis_index("exp")
    both = ("seq", "exp")
    meta = jnp.concatenate([expert_ids.astype(jnp.float32), route_weights], axis=1)
    meta = lax.all_gather(meta, "seq", axis=0, tiled=True)
    x_all = lax.all_gather(
        lax.dynamic_slice_in_dim(tokens, mine * share, share, 0), both, axis=0, tiled=True
    )
    c_all = lax.all_gather(
        lax.dynamic_slice_in_dim(cotangent, mine * share, share, 0), both, axis=0, tiled=True
    )
    match = meta[:, :top] == me.astype(jnp.float32)
    g_tok = jnp.sum(jnp.where(match, meta[:, top:], 0.0), axis=1)
    hit = jnp.any(match, axis=1)
    slabs = hit.reshape(experts, tok)
    before = (jnp.arange(tok)[:, None] < jnp.arange(tok)[None, :]).astype(jnp.bfloat16)
    within = dot(slabs.astype(jnp.bfloat16), before, ((1,), (0,))).astype(jnp.int32)
    counts = jnp.sum(slabs.astype(jnp.int32), axis=1)
    earlier = jnp.arange(experts)[None, :] < jnp.arange(experts)[:, None]
    starts = jnp.sum(jnp.where(earlier, counts[None, :], 0), axis=1)
    place = jnp.where(slabs, within + starts[:, None], -1).reshape(-1)
    pick = jnp.arange(rows, dtype=jnp.int32)[:, None] == place[None, :]
    spread = (place[:, None] == jnp.arange(rows, dtype=jnp.int32)[None, :]).astype(jnp.bfloat16)
    g_row = jnp.sum(jnp.where(pick, g_tok[None, :], 0.0), axis=1)[:, None]
    pick_b = pick.astype(jnp.bfloat16)
    wg, wu, wd = w_gate[0], w_up[0], w_down[0]

    x_rows = dot(pick_b, x_all, ((1,), (0,))).astype(jnp.bfloat16)
    gate = dot(x_rows, wg, ((1,), (0,)))
    up = dot(x_rows, wu, ((1,), (0,)))
    sigma = jax.nn.sigmoid(gate)
    silu = gate * sigma
    hidden = silu * up
    hidden_g = (hidden * g_row).astype(jnp.bfloat16)
    y_rows = dot(hidden_g, wd, ((1,), (0,))).astype(jnp.bfloat16)
    y_all = dot(spread, y_rows, ((1,), (0,))).astype(jnp.bfloat16)
    moe = lax.psum_scatter(y_all, both, scatter_dimension=0, tiled=True)

    c_rows = dot(pick_b, c_all, ((1,), (0,))).astype(jnp.bfloat16)
    d_cot = dot(c_rows, wd, ((1,), (1,)))
    d_hidden = d_cot * g_row
    d_gate = (d_hidden * up * sigma * (1.0 + gate * (1.0 - sigma))).astype(jnp.bfloat16)
    d_up = (d_hidden * silu).astype(jnp.bfloat16)
    wgt = jnp.sum(hidden * d_cot, axis=1)
    dx_rows = (dot(d_gate, wg, ((1,), (1,))) + dot(d_up, wu, ((1,), (1,)))).astype(jnp.bfloat16)
    dx_all = dot(spread, dx_rows, ((1,), (0,))).astype(jnp.bfloat16)
    dx = lax.psum_scatter(dx_all, both, scatter_dimension=0, tiled=True)

    wgt_tok = jnp.sum(jnp.where(pick, wgt[:, None], 0.0), axis=0).reshape(experts, tok)
    wgt_back = lax.all_to_all(wgt_tok, "seq", split_axis=0, concat_axis=0, tiled=True)
    named = expert_ids[:, :, None] == jnp.arange(experts, dtype=jnp.int32)[None, None, :]
    weight_grad = jnp.sum(jnp.where(named, wgt_back.T[:, None, :], 0.0), axis=2)
    weight_grad = lax.psum(weight_grad, "exp")

    g_gate = dot(x_rows, d_gate, ((0,), (0,))).astype(jnp.bfloat16)
    g_up = dot(x_rows, d_up, ((0,), (0,))).astype(jnp.bfloat16)
    g_down = dot(hidden_g, c_rows, ((0,), (0,))).astype(jnp.bfloat16)
    moe, dx = lax.all_gather((moe, dx), "exp", axis=0, tiled=True)
    return moe, dx, weight_grad, g_gate[None], g_up[None], g_down[None]


def solution(mesh):
    rows = P("seq", None)
    columns = P("seq", None, "exp")
    down = P("seq", "exp", None)
    return jax.shard_map(
        body,
        mesh=mesh,
        in_specs=(rows, rows, rows, rows, columns, columns, down),
        out_specs=(rows, rows, rows, columns, columns, down),
        check_vma=False,
    )
```

```python
import functools

import jax
import jax.numpy as jnp
from jax import lax
from jax.experimental import pallas as pl
from jax.experimental.pallas import tpu as pltpu
from jax.sharding import PartitionSpec as P

MESH = pl.DeviceIdType.MESH


def dot(left, right, dims):
    return lax.dot_general(left, right, (dims, ((), ())), preferred_element_type=jnp.float32)


def greet(n, m, me, mine):
    barrier = pltpu.get_barrier_semaphore()

    @pl.loop(1, n)
    def _(j):
        pl.semaphore_signal(
            barrier, inc=1, device_id=(lax.rem(me + j, n), mine), device_id_type=MESH
        )

    for q in range(1, m):
        pl.semaphore_signal(
            barrier, inc=1, device_id=(me, lax.rem(mine + q, m)), device_id_type=MESH
        )
    pl.semaphore_wait(barrier, n + m - 2)


def dispatch_kernel(n, m, x_in, r_in, x_out, r_out, send, recv, fsend, frecv, own):
    me = lax.axis_index("seq")
    mine = lax.axis_index("exp")
    per = n // m
    arrays = ((x_in, x_out), (r_in, r_out))
    out_first = lax.rem(mine + m * n - 2 * me, m)

    def in_first(plane):
        return lax.rem(2 * me + m - plane, m)

    def across(a, i, block, place, target):
        src, dst = arrays[a]
        return pltpu.make_async_remote_copy(
            src_ref=src.at[block],
            dst_ref=dst.at[place],
            send_sem=send.at[a, i],
            recv_sem=recv.at[a, i],
            device_id=(target, mine),
            device_id_type=MESH,
        )

    def onward(a, i, q, block):
        dst = arrays[a][1]
        return pltpu.make_async_remote_copy(
            src_ref=dst.at[block],
            dst_ref=dst.at[block],
            send_sem=fsend.at[a, i, q - 1],
            recv_sem=frecv.at[a, i, q - 1],
            device_id=(me, lax.rem(mine + q, m)),
            device_id_type=MESH,
        )

    greet(n, m, me, mine)
    for a in range(2):
        pltpu.make_async_copy(arrays[a][0].at[me], arrays[a][1].at[me], own.at[a]).start()

    for a in range(2):

        @pl.loop(0, per)
        def _(i):
            j = m * i + out_first
            target = lax.rem(me + j, n)

            @pl.when(j > 0)
            def _():
                across(a, i, target, me, target).start()

    for a in range(2):

        @pl.loop(0, per)
        def _(i):
            j = m * i + in_first(mine)
            source = lax.rem(me + n - j, n)

            @pl.when(j > 0)
            def _():
                across(a, i, source, source, source).wait_recv()
                for q in range(1, m):
                    onward(a, i, q, source).start()

    for a in range(2):

        @pl.loop(0, per)
        def _(i):
            j = m * i + out_first
            target = lax.rem(me + j, n)

            @pl.when(j > 0)
            def _():
                across(a, i, target, me, target).wait_send()

            k = m * i + in_first(mine)
            for q in range(1, m):

                @pl.when(k > 0)
                def _(q=q):
                    onward(a, i, q, lax.rem(me + n - k, n)).wait_send()

                h = m * i + in_first(lax.rem(mine + m - q, m))

                @pl.when(h > 0)
                def _(q=q, h=h):
                    onward(a, i, q, lax.rem(me + n - h, n)).wait_recv()

        pltpu.make_async_copy(arrays[a][0].at[me], arrays[a][1].at[me], own.at[a]).wait()


def dispatch(n, m, x_send, r_send):
    shape = jax.ShapeDtypeStruct(x_send.shape, x_send.dtype)
    per = n // m
    sent = x_send.size * 2
    return pl.pallas_call(
        functools.partial(dispatch_kernel, n, m),
        out_shape=(shape, shape),
        in_specs=[pl.BlockSpec(memory_space=pl.ANY)] * 2,
        out_specs=[pl.BlockSpec(memory_space=pl.ANY)] * 2,
        scratch_shapes=[
            pltpu.SemaphoreType.DMA((2, per)),
            pltpu.SemaphoreType.DMA((2, per)),
            pltpu.SemaphoreType.DMA((2, per, m - 1)),
            pltpu.SemaphoreType.DMA((2, per, m - 1)),
            pltpu.SemaphoreType.DMA((2,)),
        ],
        compiler_params=pltpu.CompilerParams(collective_id=0, has_side_effects=True),
        cost_estimate=pl.CostEstimate(flops=0, bytes_accessed=4 * sent, transcendentals=0),
    )(x_send, r_send)


def back_kernel(n, m, y_in, dx_in, y_out, dx_out, part, total, psend, precv, send, recv):
    me = lax.axis_index("seq")
    mine = lax.axis_index("exp")
    per = n // m
    arrays = ((y_in, y_out), (dx_in, dx_out))

    def slab(i, plane):
        return m * i + lax.rem(plane + m * n - me, m)

    def over(a, i, q):
        plane = lax.rem(mine + q, m)
        return pltpu.make_async_remote_copy(
            src_ref=arrays[a][0].at[slab(i, plane)],
            dst_ref=part.at[a, q - 1, i],
            send_sem=psend.at[a, q - 1, i],
            recv_sem=precv.at[a, q - 1, i],
            device_id=(me, plane),
            device_id_type=MESH,
        )

    def home(a, i, target, place):
        return pltpu.make_async_remote_copy(
            src_ref=total.at[a, i],
            dst_ref=arrays[a][1].at[place],
            send_sem=send.at[a, i],
            recv_sem=recv.at[a, place],
            device_id=(target, mine),
            device_id_type=MESH,
        )

    greet(n, m, me, mine)
    turn = me // m
    for a in range(2):

        @pl.loop(0, per)
        def _(i):
            for q in range(1, m):
                over(a, lax.rem(i + turn, per), q).start()

    for a in range(2):

        @pl.loop(0, per)
        def _(step):
            i = lax.rem(step + turn, per)
            s = slab(i, mine)
            summed = arrays[a][0][s].astype(jnp.float32)
            for q in range(1, m):
                over(a, i, q).wait_recv()
                summed = summed + part[a, q - 1, i].astype(jnp.float32)
            total[a, i] = summed.astype(jnp.bfloat16)

            @pl.when(s != me)
            def _():
                home(a, i, s, me // m).start()

            @pl.when(s == me)
            def _():
                arrays[a][1][me // m] = total[a, i]

    for a in range(2):

        @pl.loop(0, per)
        def _(i):
            for q in range(1, m):
                over(a, i, q).wait_send()
            s = slab(i, mine)

            @pl.when(s != me)
            def _():
                home(a, i, s, me // m).wait_send()
                home(a, i, s, i).wait_recv()


def back(n, m, y_part, dx_part):
    per = n // m
    block = y_part.shape[1:]
    shape = jax.ShapeDtypeStruct((per, *block), y_part.dtype)
    sent = y_part.size * 2
    return pl.pallas_call(
        functools.partial(back_kernel, n, m),
        out_shape=(shape, shape),
        in_specs=[pl.BlockSpec(memory_space=pltpu.VMEM)] * 2,
        out_specs=[pl.BlockSpec(memory_space=pltpu.VMEM)] * 2,
        scratch_shapes=[
            pltpu.VMEM((2, m - 1, per, *block), jnp.bfloat16),
            pltpu.VMEM((2, per, *block), jnp.bfloat16),
            pltpu.SemaphoreType.DMA((2, m - 1, per)),
            pltpu.SemaphoreType.DMA((2, m - 1, per)),
            pltpu.SemaphoreType.DMA((2, per)),
            pltpu.SemaphoreType.DMA((2, per)),
        ],
        compiler_params=pltpu.CompilerParams(
            collective_id=1, has_side_effects=True, vmem_limit_bytes=48 * 2**20
        ),
        cost_estimate=pl.CostEstimate(flops=0, bytes_accessed=4 * sent, transcendentals=0),
    )(y_part, dx_part)


def body(tokens, expert_ids, route_weights, cotangent, w_gate, w_up, w_down):
    tok, width = tokens.shape
    top = expert_ids.shape[1]
    n = lax.axis_size("seq")
    m = lax.axis_size("exp")
    capacity = 3 * tok * top // (2 * n)
    total = n * capacity
    me = lax.axis_index("seq")
    mine = lax.axis_index("exp")

    named = expert_ids[:, :, None] == jnp.arange(n, dtype=jnp.int32)[None, None, :]
    hits = jnp.any(named, axis=1)
    earlier = (jnp.arange(tok)[:, None] > jnp.arange(tok)[None, :]).astype(jnp.bfloat16)
    before = dot(earlier, hits.astype(jnp.bfloat16), ((1,), (0,))).astype(jnp.int32)
    slot = jnp.sum(jnp.where(named, before[:, None, :], 0), axis=2)
    target = expert_ids * capacity + slot
    rows = jnp.arange(total, dtype=jnp.int32)
    here = target.T[:, None, :] == rows[None, :, None]
    pick = jnp.any(here, axis=0).astype(jnp.bfloat16)
    g_row = jnp.sum(jnp.where(here, route_weights.T[:, None, :], 0.0), axis=(0, 2))
    x_send = dot(pick, tokens, ((1,), (0,))).astype(jnp.bfloat16)
    r_send = (dot(pick, cotangent, ((1,), (0,))) * g_row[:, None]).astype(jnp.bfloat16)
    blocks = (n, capacity, width)
    x_rows, r_rows = dispatch(n, m, x_send.reshape(blocks), r_send.reshape(blocks))
    x_rows = x_rows.reshape(total, width)
    r_rows = r_rows.reshape(total, width)

    wg, wu, wd = w_gate[0], w_up[0], w_down[0]
    gate = dot(x_rows, wg, ((1,), (0,)))
    up = dot(x_rows, wu, ((1,), (0,)))
    sigma = jax.nn.sigmoid(gate)
    silu = gate * sigma
    hidden_f = silu * up
    hidden = hidden_f.astype(jnp.bfloat16)
    y_part = dot(hidden, wd, ((1,), (0,))).astype(jnp.bfloat16)
    d_hidden = dot(r_rows, wd, ((1,), (1,)))
    d_gate = (d_hidden * up * sigma * (1.0 + gate * (1.0 - sigma))).astype(jnp.bfloat16)
    d_up = (d_hidden * silu).astype(jnp.bfloat16)
    wgt = jnp.sum(hidden_f * d_hidden, axis=1)
    dx_part = (dot(d_gate, wg, ((1,), (1,))) + dot(d_up, wu, ((1,), (1,)))).astype(jnp.bfloat16)
    y_back, dx_back = back(n, m, y_part.reshape(blocks), dx_part.reshape(blocks))

    wgt_back = lax.all_to_all(
        wgt.reshape(n, capacity), "seq", split_axis=0, concat_axis=0, tiled=True
    ).reshape(total)
    route = target[:, :, None] == rows[None, None, :]
    products = jnp.sum(jnp.where(route, wgt_back[None, None, :], 0.0), axis=2) / route_weights

    kept = total // m
    place = jnp.arange(kept, dtype=jnp.int32)
    kept_expert = place // capacity * m + lax.rem(mine + m * n - me, m)
    kept_row = kept_expert * capacity + lax.rem(place, capacity)
    kept_route = target[:, :, None] == kept_row[None, None, :]
    weight = jnp.sum(jnp.where(kept_route, route_weights[:, :, None], 0.0), axis=1)
    high = weight.astype(jnp.bfloat16)
    low = (weight - high.astype(jnp.float32)).astype(jnp.bfloat16)
    y_flat = y_back.reshape(kept, width)
    y_sum = dot(high, y_flat, ((1,), (0,))) + dot(low, y_flat, ((1,), (0,)))
    one = jnp.any(kept_route, axis=1).astype(jnp.bfloat16)
    dx_sum = dot(one, dx_back.reshape(kept, width), ((1,), (0,)))
    y_full, dx_full, weight_grad = lax.psum((y_sum, dx_sum, products), "exp")

    g_gate = dot(x_rows, d_gate, ((0,), (0,))).astype(jnp.bfloat16)
    g_up = dot(x_rows, d_up, ((0,), (0,))).astype(jnp.bfloat16)
    g_down = dot(hidden, r_rows, ((0,), (0,))).astype(jnp.bfloat16)
    return (
        y_full.astype(jnp.bfloat16),
        dx_full.astype(jnp.bfloat16),
        weight_grad,
        g_gate[None],
        g_up[None],
        g_down[None],
    )


def solution(mesh):
    rows = P("seq", None)
    columns = P("seq", None, "exp")
    down = P("seq", "exp", None)
    return jax.shard_map(
        body,
        mesh=mesh,
        in_specs=(rows, rows, rows, rows, columns, columns, down),
        out_specs=(rows, rows, rows, columns, columns, down),
        check_vma=False,
    )
```

```python
import functools

import jax
import jax.numpy as jnp
from jax import lax
from jax.experimental import pallas as pl
from jax.experimental.layout import Layout, with_layout_constraint
from jax.experimental.pallas import tpu as pltpu
from jax.sharding import PartitionSpec as P

MESH = pl.DeviceIdType.MESH


def dot(left, right, dims):
    return lax.dot_general(left, right, (dims, ((), ())), preferred_element_type=jnp.float32)


def row_major(array):
    return with_layout_constraint(array, Layout(major_to_minor=(0, 1)))


def greet(n, m, me, mine):
    barrier = pltpu.get_barrier_semaphore()

    @pl.loop(1, n)
    def _(j):
        pl.semaphore_signal(
            barrier, inc=1, device_id=(lax.rem(me + j, n), mine), device_id_type=MESH
        )

    for q in range(1, m):
        pl.semaphore_signal(
            barrier, inc=1, device_id=(me, lax.rem(mine + q, m)), device_id_type=MESH
        )
    pl.semaphore_wait(barrier, n + m - 2)


def dispatch_kernel(n, m, x_in, r_in, x_out, r_out, send, recv, fsend, frecv, own):
    me = lax.axis_index("seq")
    mine = lax.axis_index("exp")
    per = n // m
    arrays = ((x_in, x_out), (r_in, r_out))
    out_first = lax.rem(mine + m * n - 2 * me, m)

    def in_first(plane):
        return lax.rem(2 * me + m - plane, m)

    def across(a, i, block, place, target):
        src, dst = arrays[a]
        return pltpu.make_async_remote_copy(
            src_ref=src.at[block],
            dst_ref=dst.at[place],
            send_sem=send.at[a, i],
            recv_sem=recv.at[a, i],
            device_id=(target, mine),
            device_id_type=MESH,
        )

    def onward(a, i, q, block):
        dst = arrays[a][1]
        return pltpu.make_async_remote_copy(
            src_ref=dst.at[block],
            dst_ref=dst.at[block],
            send_sem=fsend.at[a, i, q - 1],
            recv_sem=frecv.at[a, i, q - 1],
            device_id=(me, lax.rem(mine + q, m)),
            device_id_type=MESH,
        )

    greet(n, m, me, mine)
    for a in range(2):
        pltpu.make_async_copy(arrays[a][0].at[me], arrays[a][1].at[me], own.at[a]).start()

    for a in range(2):

        @pl.loop(0, per)
        def _(i):
            j = m * i + out_first
            target = lax.rem(me + j, n)

            @pl.when(j > 0)
            def _():
                across(a, i, target, me, target).start()

    for a in range(2):

        @pl.loop(0, per)
        def _(i):
            j = m * i + in_first(mine)
            source = lax.rem(me + n - j, n)

            @pl.when(j > 0)
            def _():
                across(a, i, source, source, source).wait_recv()
                for q in range(1, m):
                    onward(a, i, q, source).start()

    for a in range(2):

        @pl.loop(0, per)
        def _(i):
            j = m * i + out_first
            target = lax.rem(me + j, n)

            @pl.when(j > 0)
            def _():
                across(a, i, target, me, target).wait_send()

            k = m * i + in_first(mine)
            for q in range(1, m):

                @pl.when(k > 0)
                def _(q=q):
                    onward(a, i, q, lax.rem(me + n - k, n)).wait_send()

                h = m * i + in_first(lax.rem(mine + m - q, m))

                @pl.when(h > 0)
                def _(q=q, h=h):
                    onward(a, i, q, lax.rem(me + n - h, n)).wait_recv()

        pltpu.make_async_copy(arrays[a][0].at[me], arrays[a][1].at[me], own.at[a]).wait()


def dispatch(n, m, x_send, r_send):
    shape = jax.ShapeDtypeStruct(x_send.shape, x_send.dtype)
    per = n // m
    sent = x_send.size * 2
    return pl.pallas_call(
        functools.partial(dispatch_kernel, n, m),
        out_shape=(shape, shape),
        in_specs=[pl.BlockSpec(memory_space=pl.ANY)] * 2,
        out_specs=[pl.BlockSpec(memory_space=pl.ANY)] * 2,
        scratch_shapes=[
            pltpu.SemaphoreType.DMA((2, per)),
            pltpu.SemaphoreType.DMA((2, per)),
            pltpu.SemaphoreType.DMA((2, per, m - 1)),
            pltpu.SemaphoreType.DMA((2, per, m - 1)),
            pltpu.SemaphoreType.DMA((2,)),
        ],
        compiler_params=pltpu.CompilerParams(collective_id=0, has_side_effects=True),
        cost_estimate=pl.CostEstimate(flops=0, bytes_accessed=4 * sent, transcendentals=0),
    )(x_send, r_send)


def back_kernel(n, m, y_in, dx_in, y_out, dx_out, part, total, psend, precv, send, recv):
    me = lax.axis_index("seq")
    mine = lax.axis_index("exp")
    per = n // m
    arrays = ((y_in, y_out), (dx_in, dx_out))

    def slab(i, plane):
        return m * i + lax.rem(plane + m * n - me, m)

    def over(a, i, q):
        plane = lax.rem(mine + q, m)
        return pltpu.make_async_remote_copy(
            src_ref=arrays[a][0].at[slab(i, plane)],
            dst_ref=part.at[a, q - 1, i],
            send_sem=psend.at[a, q - 1, i],
            recv_sem=precv.at[a, q - 1, i],
            device_id=(me, plane),
            device_id_type=MESH,
        )

    def home(a, i, target, place):
        return pltpu.make_async_remote_copy(
            src_ref=total.at[a, i],
            dst_ref=arrays[a][1].at[place],
            send_sem=send.at[a, i],
            recv_sem=recv.at[a, place],
            device_id=(target, mine),
            device_id_type=MESH,
        )

    greet(n, m, me, mine)
    turn = me // m
    for a in range(2):

        @pl.loop(0, per)
        def _(i):
            for q in range(1, m):
                over(a, lax.rem(i + turn, per), q).start()

    for a in range(2):

        @pl.loop(0, per)
        def _(step):
            i = lax.rem(step + turn, per)
            s = slab(i, mine)
            summed = arrays[a][0][s].astype(jnp.float32)
            for q in range(1, m):
                over(a, i, q).wait_recv()
                summed = summed + part[a, q - 1, i].astype(jnp.float32)
            total[a, i] = summed.astype(jnp.bfloat16)

            @pl.when(s != me)
            def _():
                home(a, i, s, me // m).start()

            @pl.when(s == me)
            def _():
                arrays[a][1][me // m] = total[a, i]

    for a in range(2):

        @pl.loop(0, per)
        def _(i):
            for q in range(1, m):
                over(a, i, q).wait_send()
            s = slab(i, mine)

            @pl.when(s != me)
            def _():
                home(a, i, s, me // m).wait_send()
                home(a, i, s, i).wait_recv()


def back(n, m, y_part, dx_part):
    per = n // m
    block = y_part.shape[1:]
    shape = jax.ShapeDtypeStruct((per, *block), y_part.dtype)
    sent = y_part.size * 2
    return pl.pallas_call(
        functools.partial(back_kernel, n, m),
        out_shape=(shape, shape),
        in_specs=[pl.BlockSpec(memory_space=pltpu.VMEM)] * 2,
        out_specs=[pl.BlockSpec(memory_space=pltpu.VMEM)] * 2,
        scratch_shapes=[
            pltpu.VMEM((2, m - 1, per, *block), jnp.bfloat16),
            pltpu.VMEM((2, per, *block), jnp.bfloat16),
            pltpu.SemaphoreType.DMA((2, m - 1, per)),
            pltpu.SemaphoreType.DMA((2, m - 1, per)),
            pltpu.SemaphoreType.DMA((2, per)),
            pltpu.SemaphoreType.DMA((2, per)),
        ],
        compiler_params=pltpu.CompilerParams(
            collective_id=1, has_side_effects=True, vmem_limit_bytes=48 * 2**20
        ),
        cost_estimate=pl.CostEstimate(flops=0, bytes_accessed=4 * sent, transcendentals=0),
    )(y_part, dx_part)


def body(tokens, expert_ids, route_weights, cotangent, w_gate, w_up, w_down):
    tok, width = tokens.shape
    top = expert_ids.shape[1]
    n = lax.axis_size("seq")
    m = lax.axis_size("exp")
    capacity = 3 * tok * top // (2 * n)
    total = n * capacity
    me = lax.axis_index("seq")
    mine = lax.axis_index("exp")

    named = expert_ids[:, :, None] == jnp.arange(n, dtype=jnp.int32)[None, None, :]
    hits = jnp.any(named, axis=1)
    earlier = (jnp.arange(tok)[:, None] > jnp.arange(tok)[None, :]).astype(jnp.bfloat16)
    before = dot(earlier, hits.astype(jnp.bfloat16), ((1,), (0,))).astype(jnp.int32)
    slot = jnp.sum(jnp.where(named, before[:, None, :], 0), axis=2)
    target = expert_ids * capacity + slot
    rows = jnp.arange(total, dtype=jnp.int32)
    here = target.T[:, None, :] == rows[None, :, None]
    pick = jnp.any(here, axis=0).astype(jnp.bfloat16)
    g_row = jnp.sum(jnp.where(here, route_weights.T[:, None, :], 0.0), axis=(0, 2))
    x_send = dot(pick, tokens, ((1,), (0,))).astype(jnp.bfloat16)
    r_send = (dot(pick, cotangent, ((1,), (0,))) * g_row[:, None]).astype(jnp.bfloat16)
    x_send, r_send = row_major(x_send), row_major(r_send)
    blocks = (n, capacity, width)
    x_rows, r_rows = dispatch(n, m, x_send.reshape(blocks), r_send.reshape(blocks))
    x_rows = x_rows.reshape(total, width)
    r_rows = r_rows.reshape(total, width)

    wg, wu, wd = w_gate[0], w_up[0], w_down[0]
    gate = dot(x_rows, wg, ((1,), (0,)))
    up = dot(x_rows, wu, ((1,), (0,)))
    sigma = jax.nn.sigmoid(gate)
    silu = gate * sigma
    hidden_f = silu * up
    hidden = hidden_f.astype(jnp.bfloat16)
    y_part = dot(hidden, wd, ((1,), (0,))).astype(jnp.bfloat16)
    d_hidden = dot(r_rows, wd, ((1,), (1,)))
    d_gate = (d_hidden * up * sigma * (1.0 + gate * (1.0 - sigma))).astype(jnp.bfloat16)
    d_up = (d_hidden * silu).astype(jnp.bfloat16)
    wgt = jnp.sum(hidden_f * d_hidden, axis=1)
    dx_part = (dot(d_gate, wg, ((1,), (1,))) + dot(d_up, wu, ((1,), (1,)))).astype(jnp.bfloat16)
    y_part, dx_part = row_major(y_part), row_major(dx_part)
    y_back, dx_back = back(n, m, y_part.reshape(blocks), dx_part.reshape(blocks))

    wgt_back = lax.all_to_all(
        wgt.reshape(n, capacity), "seq", split_axis=0, concat_axis=0, tiled=True
    ).reshape(total)
    route = target[:, :, None] == rows[None, None, :]
    products = jnp.sum(jnp.where(route, wgt_back[None, None, :], 0.0), axis=2) / route_weights

    kept = total // m
    place = jnp.arange(kept, dtype=jnp.int32)
    kept_expert = place // capacity * m + lax.rem(mine + m * n - me, m)
    kept_row = kept_expert * capacity + lax.rem(place, capacity)
    kept_route = target[:, :, None] == kept_row[None, None, :]
    weight = jnp.sum(jnp.where(kept_route, route_weights[:, :, None], 0.0), axis=1)
    high = weight.astype(jnp.bfloat16)
    low = (weight - high.astype(jnp.float32)).astype(jnp.bfloat16)
    y_flat = y_back.reshape(kept, width)
    y_sum = dot(high, y_flat, ((1,), (0,))) + dot(low, y_flat, ((1,), (0,)))
    one = jnp.any(kept_route, axis=1).astype(jnp.bfloat16)
    dx_sum = dot(one, dx_back.reshape(kept, width), ((1,), (0,)))
    if m == 2:
        swap = [(0, 1), (1, 0)]
        y_own, dx_own = y_sum.astype(jnp.bfloat16), dx_sum.astype(jnp.bfloat16)
        y_full = y_own.astype(jnp.float32) + lax.ppermute(y_own, "exp", swap).astype(jnp.float32)
        dx_full = dx_own.astype(jnp.float32) + lax.ppermute(dx_own, "exp", swap).astype(jnp.float32)
        weight_grad = products + lax.ppermute(products, "exp", swap)
    else:
        y_full, dx_full, weight_grad = lax.psum((y_sum, dx_sum, products), "exp")

    d_gate, d_up, hidden, y_back = lax.optimization_barrier((d_gate, d_up, hidden, y_back))
    g_gate = dot(x_rows, d_gate, ((0,), (0,))).astype(jnp.bfloat16)
    g_up = dot(x_rows, d_up, ((0,), (0,))).astype(jnp.bfloat16)
    g_down = dot(hidden, r_rows, ((0,), (0,))).astype(jnp.bfloat16)
    return (
        y_full.astype(jnp.bfloat16),
        dx_full.astype(jnp.bfloat16),
        weight_grad,
        g_gate[None],
        g_up[None],
        g_down[None],
    )


def solution(mesh):
    rows = P("seq", None)
    columns = P("seq", None, "exp")
    down = P("seq", "exp", None)
    return jax.shard_map(
        body,
        mesh=mesh,
        in_specs=(rows, rows, rows, rows, columns, columns, down),
        out_specs=(rows, rows, rows, columns, columns, down),
        check_vma=False,
    )
```
